32 devices in a mesh: col: 8 (over z, y), lev: 4 (over x, core).
Axes of the slice: x: 2, y: 2, z: 4, core: 2. Of those that a mesh axis runs over, the one named last changes fastest.
Arguments:
- fields: bfloat16 [2, 32, 8192], P(None, 'lev', 'col'), may hold values from 0.5 to 3
- bracket: int32 [8, 8192], P(None, 'col'), may hold values from 0 to 30
- fraction: float32 [8, 8192], P(None, 'col'), may hold values from 0 to 1
- remap_weights: bfloat16 [128, 128, 128], P('col'), may hold values from 0 to 0.015625
- intersections: int32 [3, 256], P(None, 'col'), may hold values from 0 to 63, as said below
- tile_owner: int32 [64], replicated, may hold values from 0 to 63, as said below
Outputs:
- normalized: float32 [2, 8, 64, 128], P(None, 'lev', 'col')
The draws below stay inside these ranges and needn't reach their ends.
Inputs may be any that keep to these rules, and one draw needn't show every extreme that they name: `intersections`: row 0 names a source block of the entry's own col index; row 1 a target tile whose owner, tile_owner[tile] // 8, lies within 2 indices of the entry's col index or exactly 4 indices away, cyclically; row 2 a weight block of the entry's own col index. `tile_owner`: A permutation of the tiles.
All inputs are finite; a program needn't handle non-finite values.
Results may differ from the reference program's by a relative error of at most 0.00031.
Values may be sent and summed in bfloat16 or wider, within the bound.
A program may use at most 64 MiB of HBM per device.

```python
import jax
import jax.numpy as jnp
from jax import lax

F = 2
LEV = 32
PLEV = 8
BLK = 128
TILE = 128
HALF = 2
BLK_DEV = 8
TILE_DEV = 8
ENT_DEV = 32
WB_DEV = 16
COLS = 8192
TILES = 64
ENT = 256
WB = 128
N_COL = 8


def intersection_layout(key):
    order = jax.random.permutation(jax.random.fold_in(key, 11), TILES).astype(jnp.int32)
    tile_at = jnp.argsort(order).astype(jnp.int32)
    entry_total = ENT_DEV * N_COL
    entry_ids = jnp.arange(entry_total, dtype=jnp.int32)
    device = entry_ids // ENT_DEV
    near = jax.random.randint(jax.random.fold_in(key, 12), (entry_total,), -HALF, HALF + 1).astype(jnp.int32)
    offset = jnp.where(entry_ids % ENT_DEV == 0, N_COL // 2, near).astype(jnp.int32)
    local_tile = jax.random.randint(jax.random.fold_in(key, 13), (entry_total,), 0, TILE_DEV).astype(jnp.int32)
    owner_dev = (device + offset + N_COL) % N_COL
    target = jnp.take(tile_at, owner_dev * TILE_DEV + local_tile)
    source = jax.random.randint(jax.random.fold_in(key, 14), (entry_total,), 0, BLK_DEV).astype(jnp.int32)
    block_id = jax.random.randint(jax.random.fold_in(key, 15), (entry_total,), 0, WB_DEV).astype(jnp.int32)
    return (order, jnp.stack([source, target, block_id]).astype(jnp.int32))


def draw_intersections(key, part):
    return intersection_layout(key)[1]


def draw_tile_owner(key, part):
    return intersection_layout(key)[0]


def plant(result, own_key, smallest, high):
    dims = result.shape
    spot = [jax.random.randint(jax.random.fold_in(own_key, axis), (), 0, dims[axis]) for axis in range(len(dims))]
    result = result.at[tuple(spot)].set(smallest)
    longest = dims.index(max(dims))
    spot[longest] = (spot[longest] + 1) % dims[longest]
    return result.at[tuple(spot)].set(high)


def steps_of(key, extent, shards, least, top_value):
    def one(axis_at, shards_of):
        steps = jax.random.uniform(jax.random.fold_in(jax.random.fold_in(key, 6), axis_at), (shards_of,), jnp.float32, least / len(shards), top_value / len(shards))
        return jnp.repeat(jnp.exp(steps), extent[axis_at] // shards_of).reshape((-1,) + (1,) * (len(extent) - axis_at - 1))

    level = one(*shards[0])
    for cut in shards[1:]:
        level = level * one(*cut)
    return level


def setup_inputs(seed: int = 0) -> dict:
    seeds = jax.random.split(jax.random.key(seed), 7)
    return {
        "fields": jnp.clip(0.5 + 2.5 * jax.random.uniform(seeds[0], (F, LEV, COLS), jnp.float32) ** steps_of(seeds[0], (F, LEV, COLS), ((1, 4), (2, 8)), -0.2, 0.2), 0.5, 3.0).astype(jnp.bfloat16),
        "bracket": plant(jax.random.randint(seeds[1], (PLEV, COLS), 0, LEV - 1), jax.random.fold_in(seeds[1], 1), 0, (LEV - 1) - 1).astype(jnp.int32),
        "fraction": jnp.clip(1.0 * jax.random.uniform(seeds[2], (PLEV, COLS), jnp.float32) ** steps_of(seeds[2], (PLEV, COLS), ((1, 8),), -0.2, 0.2), 0.0, 1.0),
        "remap_weights": jnp.clip(0.015625 * jax.random.uniform(seeds[3], (WB, BLK, TILE), jnp.float32) ** steps_of(seeds[3], (WB, BLK, TILE), ((0, 8),), -0.2, 0.2), 0.0, 0.015625).astype(jnp.bfloat16),
        "intersections": draw_intersections(jax.random.fold_in(seeds[6], 71), 0),
        "tile_owner": draw_tile_owner(jax.random.fold_in(seeds[6], 71), 0),
    }


epsilon = 1e-06

def reference(fields, bracket, fraction, remap_weights, intersections, tile_owner):
    values = fields.astype(jnp.float32)
    lower_index = jnp.broadcast_to(bracket[None], (F, PLEV, COLS))
    below_vals = jnp.take_along_axis(values, lower_index, axis=1)
    above_vals = jnp.take_along_axis(values, lower_index + 1, axis=1)
    interp = ((1.0 - fraction[None]) * below_vals + fraction[None] * above_vals).astype(jnp.bfloat16)
    blocks = interp.reshape(F, PLEV, N_COL, BLK_DEV, BLK).transpose(2, 0, 1, 3, 4)
    entry_lists = intersections.reshape(3, N_COL, ENT_DEV).transpose(1, 0, 2)
    weight_sets = remap_weights.reshape(N_COL, WB_DEV, BLK, TILE)

    def per_device(packed):
        block_set, entry_set, weight_set = packed
        chosen = jnp.take(block_set, entry_set[0], axis=2).astype(jnp.float32)
        picked = jnp.take(weight_set, entry_set[2], axis=0).astype(jnp.float32)
        return jnp.einsum('fpeb,ebt->efpt', chosen, picked, precision=lax.Precision.HIGHEST)
    parts = lax.map(per_device, (blocks, entry_lists, weight_sets))
    parts = parts.reshape(ENT, F, PLEV, TILE)
    slot_index = jnp.take(tile_owner, intersections[1])
    remapped = jax.ops.segment_sum(parts, slot_index, num_segments=TILES)
    remapped = remapped.transpose(1, 2, 0, 3)
    shifted_left = jnp.concatenate([remapped[..., :1], remapped[..., :-1]], axis=-1)
    shifted_right = jnp.concatenate([remapped[..., 1:], remapped[..., -1:]], axis=-1)
    filtered = 0.25 * shifted_left + 0.5 * remapped + 0.25 * shifted_right
    cells = float(TILES * TILE)
    field_mean = lax.optimization_barrier(jnp.sum(filtered, axis=(2, 3))) / cells
    centered = filtered - field_mean[:, :, None, None]
    field_var = lax.optimization_barrier(jnp.sum(centered * centered, axis=(2, 3))) / cells
    return centered * lax.rsqrt(field_var + epsilon)[:, :, None, None]
```

```python
import functools

import jax
import jax.numpy as jnp
from jax import lax
from jax.experimental import pallas as pl
from jax.experimental.pallas import tpu as pltpu
from jax.sharding import PartitionSpec as P

HALF = 2
EPSILON = 1e-06


def offsets_of(n_col):
    near = [n_col // 2]
    for by in range(HALF, 0, -1):
        near += [by, -by]
    found = [0]
    for by in near:
        if by % n_col not in found:
            found.append(by % n_col)
    return found


def split3(x):
    high = x.astype(jnp.bfloat16)
    rest = x - high.astype(jnp.float32)
    mid = rest.astype(jnp.bfloat16)
    low = (rest - mid.astype(jnp.float32)).astype(jnp.bfloat16)
    return high, mid, low


def kernel(
    n_col, n_lev,
    fields_hbm, bracket_hbm, fraction_hbm, weights_hbm, inter_hbm, owner_hbm,
    out_ref,
    fields_v, bracket_v, fraction_v, weights_v, inter_v, owner_v,
    lev_out, lev_in, col_out, col_in, stats,
    local_sem, lev_send, lev_recv, col_send, col_recv, stat_send, stat_recv,
):
    F, lev_dev, cols = fields_v.shape
    plev = bracket_v.shape[0]
    plev_dev = plev // n_lev
    n_wb, blk, tile = weights_v.shape
    n_src = cols // blk
    n_ent = inter_v.shape[1]
    n_tiles = owner_v.shape[1]
    tile_dev = n_tiles // n_col
    offsets = offsets_of(n_col)
    me = lax.axis_index("col")
    lv = lax.axis_index("lev")

    barrier = pltpu.get_barrier_semaphore()
    for by in range(1, n_lev):
        pl.semaphore_signal(barrier, inc=1, device_id={"lev": lax.rem(lv + by, n_lev)}, device_id_type=pl.DeviceIdType.MESH)

    def greet(by, carry):
        pl.semaphore_signal(barrier, inc=1, device_id={"col": lax.rem(me + by, n_col)}, device_id_type=pl.DeviceIdType.MESH)
        return carry

    few = n_col <= 16
    lax.fori_loop(1, n_col, greet, 0, unroll=few)

    pairs = [(fields_hbm, fields_v), (bracket_hbm, bracket_v), (fraction_hbm, fraction_v),
             (inter_hbm, inter_v), (owner_hbm, owner_v), (weights_hbm, weights_v)]
    loads = [pltpu.make_async_copy(src, dst, local_sem.at[i]) for i, (src, dst) in enumerate(pairs)]
    for load in loads:
        load.start()

    for load in loads[:3]:
        load.wait()
    first = lv * lev_dev
    for s in range(n_src):
        here = slice(s * blk, (s + 1) * blk)
        lower = bracket_v[:, here] - first
        up = fraction_v[:, here]
        down = 1.0 - up
        sums = [None] * F
        values = [fields_v[f, :, here].astype(jnp.float32) for f in range(F)]
        for l in range(lev_dev):
            coef = jnp.where(lower == l, down, jnp.where(lower == l - 1, up, 0.0))
            for f in range(F):
                term = coef * values[f][l : l + 1, :]
                sums[f] = term if sums[f] is None else sums[f] + term
        for f in range(F):
            lev_out[:, f, s, :] = sums[f]

    pl.semaphore_wait(barrier, n_lev - 1 + n_col - 1)

    lev_copies = []
    for by in range(1, n_lev):
        to = lax.rem(lv + by, n_lev)
        lev_copies.append(pltpu.make_async_remote_copy(
            src_ref=lev_out.at[pl.ds(to * plev_dev, plev_dev)],
            dst_ref=lev_in.at[by - 1],
            send_sem=lev_send.at[by - 1],
            recv_sem=lev_recv.at[by - 1],
            device_id={"lev": to},
            device_id_type=pl.DeviceIdType.MESH,
        ))
    for copy in lev_copies:
        copy.start()

    loads[3].wait()
    loads[4].wait()
    rows = len(offsets) * tile_dev
    row = lax.broadcasted_iota(jnp.int32, (rows, n_tiles), 0)
    slot = jnp.zeros((rows, n_tiles), jnp.int32)
    for k, by in enumerate(offsets):
        base = lax.rem(me + by, n_col) * tile_dev - k * tile_dev
        slot = jnp.where((row >= k * tile_dev) & (row < (k + 1) * tile_dev), row + base, slot)
    one, nil = jnp.float32(1.0), jnp.float32(0.0)
    placed = jnp.where(slot == owner_v[...], one, nil).astype(jnp.bfloat16)
    tile_of = lax.broadcasted_iota(jnp.int32, (n_tiles, n_ent), 0) == inter_v[1:2, :]
    goes = jnp.dot(placed, jnp.where(tile_of, one, nil).astype(jnp.bfloat16), preferred_element_type=jnp.float32)
    pair_of = lax.broadcasted_iota(jnp.int32, (n_wb * n_src, n_ent), 0) == inter_v[2:3, :] * n_src + inter_v[0:1, :]
    counts = lax.dot_general(
        goes.astype(jnp.bfloat16), jnp.where(pair_of, one, nil).astype(jnp.bfloat16),
        (((1,), (1,)), ((), ())), preferred_element_type=jnp.float32,
    ).astype(jnp.bfloat16)
    counts = jnp.concatenate([counts] * 3, axis=1)
    loads[5].wait()

    interp = lev_out[pl.ds(lv * plev_dev, plev_dev)]
    for by, copy in enumerate(lev_copies):
        copy.wait_recv()
        interp = interp + lev_in[by]
    fp = plev_dev * F
    interp = interp.reshape(fp * n_src, blk).astype(jnp.bfloat16)
    products = []
    for w in range(n_wb):
        product = jnp.dot(interp, weights_v[w], preferred_element_type=jnp.float32)
        products.append(jnp.concatenate([product[i * n_src : (i + 1) * n_src] for i in range(fp)], axis=1))
    products = jnp.concatenate(split3(jnp.concatenate(products, axis=0)), axis=0)
    tiles = jnp.dot(counts, products, preferred_element_type=jnp.float32)
    for k in range(len(offsets)):
        col_out[k] = tiles[k * tile_dev : (k + 1) * tile_dev]
    col_copies = []
    for k in range(1, len(offsets)):
        col_copies.append(pltpu.make_async_remote_copy(
            src_ref=col_out.at[k],
            dst_ref=col_in.at[k - 1],
            send_sem=col_send.at[k - 1],
            recv_sem=col_recv.at[k - 1],
            device_id={"col": lax.rem(me + offsets[k], n_col)},
            device_id_type=pl.DeviceIdType.MESH,
        ))
        col_copies[-1].start()
    remapped = col_out[0]
    for k, copy in enumerate(col_copies):
        copy.wait_recv()
        remapped = remapped + col_in[k]

    lane = lax.broadcasted_iota(jnp.int32, (tile_dev, tile), 1)
    filtered = []
    for i in range(fp):
        x = remapped[:, i * tile : (i + 1) * tile]
        left = jnp.where(lane == 0, x, pltpu.roll(x, 1, 1))
        right = jnp.where(lane == tile - 1, x, pltpu.roll(x, tile - 1, 1))
        y = 0.25 * left + 0.5 * x + 0.25 * right
        filtered.append(y)
        total = jnp.sum(y, axis=0, keepdims=True)
        off = y - total * (1.0 / tile_dev)
        stats[0, i : i + 1, :] = total
        stats[0, fp + i : fp + i + 1, :] = jnp.sum(off * off, axis=0, keepdims=True)

    def stat_copy(by):
        return pltpu.make_async_remote_copy(
            src_ref=stats.at[0],
            dst_ref=stats.at[by],
            send_sem=stat_send.at[by],
            recv_sem=stat_recv.at[by],
            device_id={"col": lax.rem(me + by, n_col)},
            device_id_type=pl.DeviceIdType.MESH,
        )

    def send_stat(by, carry):
        stat_copy(by).start()
        return carry

    def take_stat(by, carry):
        stat_copy(by).wait_recv()
        return carry

    def end_stat(by, carry):
        stat_copy(by).wait_send()
        return carry

    lax.fori_loop(1, n_col, send_stat, 0, unroll=few)
    for copy in lev_copies + col_copies:
        copy.wait_send()
    lax.fori_loop(1, n_col, take_stat, 0, unroll=few)
    cells = 1.0 / float(tile_dev * tile * n_col)
    every = stats[...]
    sums = every[:, :fp]
    mean = jnp.sum(jnp.sum(sums, axis=0), axis=1, keepdims=True) * cells
    away = sums * (1.0 / tile_dev) - mean
    squares = jnp.sum(every[:, fp:], axis=0) + float(tile_dev) * jnp.sum(away * away, axis=0)
    scale = lax.rsqrt(jnp.sum(squares, axis=1, keepdims=True) * cells + EPSILON)
    for i in range(fp):
        p, f = divmod(i, F)
        out_ref[f, p] = (filtered[i] - mean[i : i + 1]) * scale[i : i + 1]
    lax.fori_loop(1, n_col, end_stat, 0, unroll=few)


def solution(mesh):
    n_col, n_lev = mesh.shape["col"], mesh.shape["lev"]

    def per_device(fields, bracket, fraction, remap_weights, intersections, tile_owner):
        F, lev_dev, cols = fields.shape
        plev = bracket.shape[0]
        plev_dev = plev // n_lev
        n_wb, blk, tile = remap_weights.shape
        n_src = cols // blk
        n_tiles = tile_owner.shape[0]
        tile_dev = n_tiles // n_col
        fp = plev_dev * F
        others = len(offsets_of(n_col)) - 1
        f32 = jnp.float32
        dma = pltpu.SemaphoreType.DMA
        return pl.pallas_call(
            functools.partial(kernel, n_col, n_lev),
            out_shape=jax.ShapeDtypeStruct((F, plev_dev, tile_dev, tile), f32),
            in_specs=[pl.BlockSpec(memory_space=pl.ANY)] * 6,
            out_specs=pl.BlockSpec(memory_space=pltpu.VMEM),
            scratch_shapes=[
                pltpu.VMEM(fields.shape, fields.dtype),
                pltpu.VMEM(bracket.shape, bracket.dtype),
                pltpu.VMEM(fraction.shape, fraction.dtype),
                pltpu.VMEM(remap_weights.shape, remap_weights.dtype),
                pltpu.VMEM(intersections.shape, intersections.dtype),
                pltpu.VMEM((1, n_tiles), tile_owner.dtype),
                pltpu.VMEM((plev, F, n_src, blk), f32),
                pltpu.VMEM((n_lev - 1, plev_dev, F, n_src, blk), f32),
                pltpu.VMEM((others + 1, tile_dev, fp * tile), f32),
                pltpu.VMEM((others, tile_dev, fp * tile), f32),
                pltpu.VMEM((n_col, 2 * fp, tile), f32),
                dma((6,)),
                dma((n_lev - 1,)),
                dma((n_lev - 1,)),
                dma((others,)),
                dma((others,)),
                dma((n_col,)),
                dma((n_col,)),
            ],
            compiler_params=pltpu.CompilerParams(collective_id=0, has_side_effects=True),
        )(fields, bracket, fraction, remap_weights, intersections, tile_owner.reshape(1, n_tiles))

    in_specs = (
        P(None, "lev", "col"),
        P(None, "col"),
        P(None, "col"),
        P("col", None, None),
        P(None, "col"),
        P(),
    )
    return jax.shard_map(
        per_device, mesh=mesh, in_specs=in_specs, out_specs=P(None, "lev", "col", None), check_vma=False
    )
```

```python
import functools

import jax
import jax.numpy as jnp
from jax import lax
from jax.experimental import pallas as pl
from jax.experimental.pallas import tpu as pltpu
from jax.sharding import PartitionSpec as P

HALF = 2
EPSILON = 1e-06


def offsets_of(n_col):
    near = [n_col // 2]
    for by in range(HALF, 0, -1):
        near += [by, -by]
    found = [0]
    for by in near:
        if by % n_col not in found:
            found.append(by % n_col)
    return found


def split3(x):
    high = x.astype(jnp.bfloat16)
    rest = x - high.astype(jnp.float32)
    mid = rest.astype(jnp.bfloat16)
    low = (rest - mid.astype(jnp.float32)).astype(jnp.bfloat16)
    return high, mid, low


def kernel(
    n_col, n_lev,
    fields_hbm, bracket_hbm, fraction_hbm, weights_hbm, inter_hbm, owner_hbm,
    out_ref,
    fields_v, bracket_v, fraction_v, weights_v, inter_v, owner_v,
    lev_out, lev_in, col_out, col_in, stats,
    local_sem, lev_send, lev_recv, col_send, col_recv, stat_send, stat_recv, relay,
):
    F, lev_dev, cols = fields_v.shape
    plev = bracket_v.shape[0]
    plev_dev = plev // n_lev
    n_wb, blk, tile = weights_v.shape
    n_src = cols // blk
    n_ent = inter_v.shape[1]
    n_tiles = owner_v.shape[1]
    tile_dev = n_tiles // n_col
    offsets = offsets_of(n_col)
    me = lax.axis_index("col")
    lv = lax.axis_index("lev")

    barrier = pltpu.get_barrier_semaphore()
    for by in range(1, n_lev):
        pl.semaphore_signal(barrier, inc=1, device_id={"lev": lax.rem(lv + by, n_lev)}, device_id_type=pl.DeviceIdType.MESH)

    few = n_col <= 16 and n_col % 2 == 0
    hops = n_col // 2

    def tell(sem):
        for there, to in (
            (me >= 0, me + 1 - 2 * lax.rem(me, 2)), (me >= 2, me - 2), (me < n_col - 2, me + 2)
        ):
            @pl.when(there)
            def _():
                pl.semaphore_signal(sem, inc=1, device_id={"col": to}, device_id_type=pl.DeviceIdType.MESH)

    def greet(by, carry):
        pl.semaphore_signal(barrier, inc=1, device_id={"col": lax.rem(me + by, n_col)}, device_id_type=pl.DeviceIdType.MESH)
        return carry

    if few:
        greeted = 1 + jnp.where(me >= 2, 1, 0) + jnp.where(me < n_col - 2, 1, 0)
        tell(barrier)
    else:
        greeted = n_col - 1
        lax.fori_loop(1, n_col, greet, 0)

    pairs = [(fields_hbm, fields_v), (bracket_hbm, bracket_v), (fraction_hbm, fraction_v),
             (inter_hbm, inter_v), (owner_hbm, owner_v), (weights_hbm, weights_v)]
    loads = [pltpu.make_async_copy(src, dst, local_sem.at[i]) for i, (src, dst) in enumerate(pairs)]
    for load in loads:
        load.start()

    for load in loads[:3]:
        load.wait()
    first = lv * lev_dev
    for s in range(n_src):
        here = slice(s * blk, (s + 1) * blk)
        lower = bracket_v[:, here] - first
        up = fraction_v[:, here]
        down = 1.0 - up
        sums = [None] * F
        values = [fields_v[f, :, here].astype(jnp.float32) for f in range(F)]
        for l in range(lev_dev):
            coef = jnp.where(lower == l, down, jnp.where(lower == l - 1, up, 0.0))
            for f in range(F):
                term = coef * values[f][l : l + 1, :]
                sums[f] = term if sums[f] is None else sums[f] + term
        for f in range(F):
            lev_out[:, f, s, :] = sums[f]

    pl.semaphore_wait(barrier, n_lev - 1 + greeted)

    lev_copies = []
    for by in range(1, n_lev):
        to = lax.rem(lv + by, n_lev)
        lev_copies.append(pltpu.make_async_remote_copy(
            src_ref=lev_out.at[pl.ds(to * plev_dev, plev_dev)],
            dst_ref=lev_in.at[by - 1],
            send_sem=lev_send.at[by - 1],
            recv_sem=lev_recv.at[by - 1],
            device_id={"lev": to},
            device_id_type=pl.DeviceIdType.MESH,
        ))
    for copy in lev_copies:
        copy.start()
    if few and hops > 1:
        tell(relay.at[0])

    loads[3].wait()
    loads[4].wait()
    rows = len(offsets) * tile_dev
    row = lax.broadcasted_iota(jnp.int32, (rows, n_tiles), 0)
    slot = jnp.zeros((rows, n_tiles), jnp.int32)
    for k, by in enumerate(offsets):
        base = lax.rem(me + by, n_col) * tile_dev - k * tile_dev
        slot = jnp.where((row >= k * tile_dev) & (row < (k + 1) * tile_dev), row + base, slot)
    one, nil = jnp.float32(1.0), jnp.float32(0.0)
    placed = jnp.where(slot == owner_v[...], one, nil).astype(jnp.bfloat16)
    tile_of = lax.broadcasted_iota(jnp.int32, (n_tiles, n_ent), 0) == inter_v[1:2, :]
    goes = jnp.dot(placed, jnp.where(tile_of, one, nil).astype(jnp.bfloat16), preferred_element_type=jnp.float32)
    pair_of = lax.broadcasted_iota(jnp.int32, (n_wb * n_src, n_ent), 0) == inter_v[2:3, :] * n_src + inter_v[0:1, :]
    counts = lax.dot_general(
        goes.astype(jnp.bfloat16), jnp.where(pair_of, one, nil).astype(jnp.bfloat16),
        (((1,), (1,)), ((), ())), preferred_element_type=jnp.float32,
    ).astype(jnp.bfloat16)
    counts = jnp.concatenate([counts] * 3, axis=1)
    loads[5].wait()

    if few:
        for hop in range(1, hops - 1):
            pl.semaphore_wait(relay.at[hop - 1], greeted)
            tell(relay.at[hop])

    interp = lev_out[pl.ds(lv * plev_dev, plev_dev)]
    for by, copy in enumerate(lev_copies):
        copy.wait_recv()
        interp = interp + lev_in[by]
    fp = plev_dev * F
    interp = interp.reshape(fp * n_src, blk).astype(jnp.bfloat16)
    products = []
    for w in range(n_wb):
        product = jnp.dot(interp, weights_v[w], preferred_element_type=jnp.float32)
        products.append(jnp.concatenate([product[i * n_src : (i + 1) * n_src] for i in range(fp)], axis=1))
    products = jnp.concatenate(split3(jnp.concatenate(products, axis=0)), axis=0)
    tiles = jnp.dot(counts, products, preferred_element_type=jnp.float32)
    for k in range(len(offsets)):
        col_out[k] = tiles[k * tile_dev : (k + 1) * tile_dev]
    if few and hops > 1:
        pl.semaphore_wait(relay.at[hops - 2], greeted)
    col_copies = []
    for k in range(1, len(offsets)):
        col_copies.append(pltpu.make_async_remote_copy(
            src_ref=col_out.at[k],
            dst_ref=col_in.at[k - 1],
            send_sem=col_send.at[k - 1],
            recv_sem=col_recv.at[k - 1],
            device_id={"col": lax.rem(me + offsets[k], n_col)},
            device_id_type=pl.DeviceIdType.MESH,
        ))
        col_copies[-1].start()
    remapped = col_out[0]
    for k, copy in enumerate(col_copies):
        copy.wait_recv()
        remapped = remapped + col_in[k]

    lane = lax.broadcasted_iota(jnp.int32, (tile_dev, tile), 1)
    filtered = []
    for i in range(fp):
        x = remapped[:, i * tile : (i + 1) * tile]
        left = jnp.where(lane == 0, x, pltpu.roll(x, 1, 1))
        right = jnp.where(lane == tile - 1, x, pltpu.roll(x, tile - 1, 1))
        y = 0.25 * left + 0.5 * x + 0.25 * right
        filtered.append(y)
        total = jnp.sum(y, axis=0, keepdims=True)
        off = y - total * (1.0 / tile_dev)
        stats[0, i : i + 1, :] = total
        stats[0, fp + i : fp + i + 1, :] = jnp.sum(off * off, axis=0, keepdims=True)

    def stat_copy(by):
        return pltpu.make_async_remote_copy(
            src_ref=stats.at[0],
            dst_ref=stats.at[by],
            send_sem=stat_send.at[by],
            recv_sem=stat_recv.at[by],
            device_id={"col": lax.rem(me + by, n_col)},
            device_id_type=pl.DeviceIdType.MESH,
        )

    def send_stat(by, carry):
        stat_copy(by).start()
        return carry

    def take_stat(by, carry):
        stat_copy(by).wait_recv()
        return carry

    def end_stat(by, carry):
        stat_copy(by).wait_send()
        return carry

    lax.fori_loop(1, n_col, send_stat, 0, unroll=few)
    for copy in lev_copies + col_copies:
        copy.wait_send()
    lax.fori_loop(1, n_col, take_stat, 0, unroll=few)
    cells = 1.0 / float(tile_dev * tile * n_col)
    every = stats[...]
    sums = every[:, :fp]
    mean = jnp.sum(jnp.sum(sums, axis=0), axis=1, keepdims=True) * cells
    away = sums * (1.0 / tile_dev) - mean
    squares = jnp.sum(every[:, fp:], axis=0) + float(tile_dev) * jnp.sum(away * away, axis=0)
    scale = lax.rsqrt(jnp.sum(squares, axis=1, keepdims=True) * cells + EPSILON)
    for i in range(fp):
        p, f = divmod(i, F)
        at = (f * plev_dev + p) * tile_dev
        out_ref[at : at + tile_dev] = (filtered[i] - mean[i : i + 1]) * scale[i : i + 1]
    lax.fori_loop(1, n_col, end_stat, 0, unroll=few)


def solution(mesh):
    n_col, n_lev = mesh.shape["col"], mesh.shape["lev"]

    def per_device(fields, bracket, fraction, remap_weights, intersections, tile_owner):
        F, lev_dev, cols = fields.shape
        plev = bracket.shape[0]
        plev_dev = plev // n_lev
        n_wb, blk, tile = remap_weights.shape
        n_src = cols // blk
        n_tiles = tile_owner.shape[0]
        tile_dev = n_tiles // n_col
        fp = plev_dev * F
        others = len(offsets_of(n_col)) - 1
        f32 = jnp.float32
        dma = pltpu.SemaphoreType.DMA
        return pl.pallas_call(
            functools.partial(kernel, n_col, n_lev),
            out_shape=pltpu.VMEM((F * plev_dev * tile_dev, tile), f32),
            in_specs=[pl.BlockSpec(memory_space=pl.ANY)] * 6,
            out_specs=pl.BlockSpec(memory_space=pltpu.VMEM),
            scratch_shapes=[
                pltpu.VMEM(fields.shape, fields.dtype),
                pltpu.VMEM(bracket.shape, bracket.dtype),
                pltpu.VMEM(fraction.shape, fraction.dtype),
                pltpu.VMEM(remap_weights.shape, remap_weights.dtype),
                pltpu.VMEM(intersections.shape, intersections.dtype),
                pltpu.VMEM((1, n_tiles), tile_owner.dtype),
                pltpu.VMEM((plev, F, n_src, blk), f32),
                pltpu.VMEM((n_lev - 1, plev_dev, F, n_src, blk), f32),
                pltpu.VMEM((others + 1, tile_dev, fp * tile), f32),
                pltpu.VMEM((others, tile_dev, fp * tile), f32),
                pltpu.VMEM((n_col, 2 * fp, tile), f32),
                dma((6,)),
                dma((n_lev - 1,)),
                dma((n_lev - 1,)),
                dma((others,)),
                dma((others,)),
                dma((n_col,)),
                dma((n_col,)),
                pltpu.SemaphoreType.REGULAR((max(n_col // 2 - 1, 1) if n_col <= 16 else 1,)),
            ],
            compiler_params=pltpu.CompilerParams(collective_id=0, has_side_effects=True),
        )(fields, bracket, fraction, remap_weights, intersections, tile_owner.reshape(1, n_tiles)).reshape(F, plev_dev, tile_dev, tile)

    in_specs = (
        P(None, "lev", "col"),
        P(None, "col"),
        P(None, "col"),
        P("col", None, None),
        P(None, "col"),
        P(),
    )
    return jax.shard_map(
        per_device, mesh=mesh, in_specs=in_specs, out_specs=P(None, "lev", "col", None), check_vma=False
    )
```

```python
import functools

import jax
import jax.numpy as jnp
from jax import lax
from jax.experimental import pallas as pl
from jax.experimental.pallas import tpu as pltpu
from jax.sharding import PartitionSpec as P

HALF = 2
EPSILON = 1e-06


def offsets_of(n_col):
    near = []
    for by in range(1, HALF + 1):
        near += [by, -by]
    near.append(n_col // 2)
    found = [0]
    for by in near:
        if by % n_col not in found:
            found.append(by % n_col)
    return found


def split3(x):
    high = x.astype(jnp.bfloat16)
    rest = x - high.astype(jnp.float32)
    mid = rest.astype(jnp.bfloat16)
    low = (rest - mid.astype(jnp.float32)).astype(jnp.bfloat16)
    return high, mid, low


def kernel(
    n_col, n_lev,
    fields_hbm, bracket_hbm, fraction_hbm, weights_hbm, inter_hbm, owner_hbm,
    out_ref,
    fields_v, bracket_v, fraction_v, weights_v, inter_v, owner_v,
    lev_out, lev_in, col_out, col_in, stats,
    local_sem, lev_send, lev_recv, col_send, col_recv, stat_send, stat_recv, relay,
):
    F, lev_dev, cols = fields_v.shape
    plev = bracket_v.shape[0]
    plev_dev = plev // n_lev
    n_wb, blk, tile = weights_v.shape
    n_src = cols // blk
    n_ent = inter_v.shape[1]
    n_tiles = owner_v.shape[1]
    tile_dev = n_tiles // n_col
    offsets = offsets_of(n_col)
    me = lax.axis_index("col")
    lv = lax.axis_index("lev")

    pairs = [(fields_hbm, fields_v), (bracket_hbm, bracket_v), (fraction_hbm, fraction_v),
             (inter_hbm, inter_v), (owner_hbm, owner_v), (weights_hbm, weights_v)]
    loads = [pltpu.make_async_copy(src, dst, local_sem.at[i]) for i, (src, dst) in enumerate(pairs)]
    for load in loads[:3]:
        load.start()

    barrier = pltpu.get_barrier_semaphore()
    for by in range(1, n_lev):
        pl.semaphore_signal(barrier, inc=1, device_id={"lev": lax.rem(lv + by, n_lev)}, device_id_type=pl.DeviceIdType.MESH)

    few = n_col <= 16 and n_col % 2 == 0
    hops = n_col // 2

    def tell(sem):
        for there, to in (
            (me >= 0, me + 1 - 2 * lax.rem(me, 2)), (me >= 2, me - 2), (me < n_col - 2, me + 2)
        ):
            @pl.when(there)
            def _():
                pl.semaphore_signal(sem, inc=1, device_id={"col": to}, device_id_type=pl.DeviceIdType.MESH)

    def greet(by, carry):
        pl.semaphore_signal(barrier, inc=1, device_id={"col": lax.rem(me + by, n_col)}, device_id_type=pl.DeviceIdType.MESH)
        return carry

    if few:
        greeted = 1 + jnp.where(me >= 2, 1, 0) + jnp.where(me < n_col - 2, 1, 0)
        tell(barrier)
    else:
        greeted = n_col - 1
        lax.fori_loop(1, n_col, greet, 0)

    for load in loads[3:]:
        load.start()

    for load in loads[:3]:
        load.wait()
    first = lv * lev_dev
    for s in range(n_src):
        here = slice(s * blk, (s + 1) * blk)
        lower = bracket_v[:, here] - first
        up = fraction_v[:, here]
        down = 1.0 - up
        sums = [None] * F
        values = [fields_v[f, :, here].astype(jnp.float32) for f in range(F)]
        for l in range(lev_dev):
            coef = jnp.where(lower == l, down, jnp.where(lower == l - 1, up, 0.0))
            for f in range(F):
                term = coef * values[f][l : l + 1, :]
                sums[f] = term if sums[f] is None else sums[f] + term
        for f in range(F):
            lev_out[:, f, s, :] = sums[f]

    pl.semaphore_wait(barrier, n_lev - 1 + greeted)

    lev_copies = []
    for by in range(1, n_lev):
        to = lax.rem(lv + by, n_lev)
        lev_copies.append(pltpu.make_async_remote_copy(
            src_ref=lev_out.at[pl.ds(to * plev_dev, plev_dev)],
            dst_ref=lev_in.at[by - 1],
            send_sem=lev_send.at[by - 1],
            recv_sem=lev_recv.at[by - 1],
            device_id={"lev": to},
            device_id_type=pl.DeviceIdType.MESH,
        ))
    for by in sorted(range(1, n_lev), key=lambda by: -min(by, n_lev - by)):
        lev_copies[by - 1].start()
    if few and hops > 1:
        tell(relay.at[0])

    loads[3].wait()
    loads[4].wait()
    rows = len(offsets) * tile_dev
    row = lax.broadcasted_iota(jnp.int32, (rows, n_tiles), 0)
    slot = jnp.zeros((rows, n_tiles), jnp.int32)
    for k, by in enumerate(offsets):
        base = lax.rem(me + by, n_col) * tile_dev - k * tile_dev
        slot = jnp.where((row >= k * tile_dev) & (row < (k + 1) * tile_dev), row + base, slot)
    one, nil = jnp.float32(1.0), jnp.float32(0.0)
    placed = jnp.where(slot == owner_v[...], one, nil).astype(jnp.bfloat16)
    tile_of = lax.broadcasted_iota(jnp.int32, (n_tiles, n_ent), 0) == inter_v[1:2, :]
    goes = jnp.dot(placed, jnp.where(tile_of, one, nil).astype(jnp.bfloat16), preferred_element_type=jnp.float32)
    pair_of = lax.broadcasted_iota(jnp.int32, (n_wb * n_src, n_ent), 0) == inter_v[2:3, :] * n_src + inter_v[0:1, :]
    counts = lax.dot_general(
        goes.astype(jnp.bfloat16), jnp.where(pair_of, one, nil).astype(jnp.bfloat16),
        (((1,), (1,)), ((), ())), preferred_element_type=jnp.float32,
    ).astype(jnp.bfloat16)
    counts = jnp.concatenate([counts] * 3, axis=1)
    loads[5].wait()

    if few:
        for hop in range(1, hops - 1):
            pl.semaphore_wait(relay.at[hop - 1], greeted)
            tell(relay.at[hop])

    interp = lev_out[pl.ds(lv * plev_dev, plev_dev)]
    for by, copy in enumerate(lev_copies):
        copy.wait_recv()
        interp = interp + lev_in[by]
    fp = plev_dev * F
    interp = interp.reshape(fp * n_src, blk).astype(jnp.bfloat16)
    products = []
    for w in range(n_wb):
        product = jnp.dot(interp, weights_v[w], preferred_element_type=jnp.float32)
        products.append(jnp.concatenate([product[i * n_src : (i + 1) * n_src] for i in range(fp)], axis=1))
    products = jnp.concatenate(split3(jnp.concatenate(products, axis=0)), axis=0)
    tiles = jnp.dot(counts, products, preferred_element_type=jnp.float32)
    for k in range(len(offsets)):
        col_out[k] = tiles[k * tile_dev : (k + 1) * tile_dev]
    if few and hops > 1:
        pl.semaphore_wait(relay.at[hops - 2], greeted)
    col_copies = []
    for k in range(1, len(offsets)):
        col_copies.append(pltpu.make_async_remote_copy(
            src_ref=col_out.at[k],
            dst_ref=col_in.at[k - 1],
            send_sem=col_send.at[k - 1],
            recv_sem=col_recv.at[k - 1],
            device_id={"col": lax.rem(me + offsets[k], n_col)},
            device_id_type=pl.DeviceIdType.MESH,
        ))
        col_copies[-1].start()
    remapped = col_out[0]
    for k, copy in enumerate(col_copies):
        copy.wait_recv()
        remapped = remapped + col_in[k]

    lane = lax.broadcasted_iota(jnp.int32, (tile_dev, tile), 1)
    filtered = []
    for i in range(fp):
        x = remapped[:, i * tile : (i + 1) * tile]
        left = jnp.where(lane == 0, x, pltpu.roll(x, 1, 1))
        right = jnp.where(lane == tile - 1, x, pltpu.roll(x, tile - 1, 1))
        y = 0.25 * left + 0.5 * x + 0.25 * right
        filtered.append(y)
        total = jnp.sum(y, axis=0, keepdims=True)
        off = y - total * (1.0 / tile_dev)
        stats[0, i : i + 1, :] = total
        stats[0, fp + i : fp + i + 1, :] = jnp.sum(off * off, axis=0, keepdims=True)

    def stat_copy(by):
        return pltpu.make_async_remote_copy(
            src_ref=stats.at[0],
            dst_ref=stats.at[by],
            send_sem=stat_send.at[by],
            recv_sem=stat_recv.at[by],
            device_id={"col": lax.rem(me + by, n_col)},
            device_id_type=pl.DeviceIdType.MESH,
        )

    def send_stat(by, carry):
        stat_copy(by).start()
        return carry

    def take_stat(by, carry):
        stat_copy(by).wait_recv()
        return carry

    def end_stat(by, carry):
        stat_copy(by).wait_send()
        return carry

    lax.fori_loop(1, n_col, send_stat, 0, unroll=few)
    for copy in lev_copies + col_copies:
        copy.wait_send()
    lax.fori_loop(1, n_col, take_stat, 0, unroll=few)
    cells = 1.0 / float(tile_dev * tile * n_col)
    every = stats[...]
    sums = every[:, :fp]
    mean = jnp.sum(jnp.sum(sums, axis=0), axis=1, keepdims=True) * cells
    away = sums * (1.0 / tile_dev) - mean
    squares = jnp.sum(every[:, fp:], axis=0) + float(tile_dev) * jnp.sum(away * away, axis=0)
    scale = lax.rsqrt(jnp.sum(squares, axis=1, keepdims=True) * cells + EPSILON)
    for i in range(fp):
        p, f = divmod(i, F)
        at = (f * plev_dev + p) * tile_dev
        out_ref[at : at + tile_dev] = (filtered[i] - mean[i : i + 1]) * scale[i : i + 1]
    lax.fori_loop(1, n_col, end_stat, 0, unroll=few)


def solution(mesh):
    n_col, n_lev = mesh.shape["col"], mesh.shape["lev"]

    def per_device(fields, bracket, fraction, remap_weights, intersections, tile_owner):
        F, lev_dev, cols = fields.shape
        plev = bracket.shape[0]
        plev_dev = plev // n_lev
        n_wb, blk, tile = remap_weights.shape
        n_src = cols // blk
        n_tiles = tile_owner.shape[0]
        tile_dev = n_tiles // n_col
        fp = plev_dev * F
        others = len(offsets_of(n_col)) - 1
        f32 = jnp.float32
        dma = pltpu.SemaphoreType.DMA
        return pl.pallas_call(
            functools.partial(kernel, n_col, n_lev),
            out_shape=pltpu.VMEM((F * plev_dev * tile_dev, tile), f32),
            in_specs=[pl.BlockSpec(memory_space=pl.ANY)] * 6,
            out_specs=pl.BlockSpec(memory_space=pltpu.VMEM),
            scratch_shapes=[
                pltpu.VMEM(fields.shape, fields.dtype),
                pltpu.VMEM(bracket.shape, bracket.dtype),
                pltpu.VMEM(fraction.shape, fraction.dtype),
                pltpu.VMEM(remap_weights.shape, remap_weights.dtype),
                pltpu.VMEM(intersections.shape, intersections.dtype),
                pltpu.VMEM((1, n_tiles), tile_owner.dtype),
                pltpu.VMEM((plev, F, n_src, blk), f32),
                pltpu.VMEM((n_lev - 1, plev_dev, F, n_src, blk), f32),
                pltpu.VMEM((others + 1, tile_dev, fp * tile), f32),
                pltpu.VMEM((others, tile_dev, fp * tile), f32),
                pltpu.VMEM((n_col, 2 * fp, tile), f32),
                dma((6,)),
                dma((n_lev - 1,)),
                dma((n_lev - 1,)),
                dma((others,)),
                dma((others,)),
                dma((n_col,)),
                dma((n_col,)),
                pltpu.SemaphoreType.REGULAR((max(n_col // 2 - 1, 1) if n_col <= 16 else 1,)),
            ],
            compiler_params=pltpu.CompilerParams(collective_id=0, has_side_effects=True),
        )(fields, bracket, fraction, remap_weights, intersections, tile_owner.reshape(1, n_tiles)).reshape(F, plev_dev, tile_dev, tile)

    in_specs = (
        P(None, "lev", "col"),
        P(None, "col"),
        P(None, "col"),
        P("col", None, None),
        P(None, "col"),
        P(),
    )
    return jax.shard_map(
        per_device, mesh=mesh, in_specs=in_specs, out_specs=P(None, "lev", "col", None), check_vma=False
    )
```
